32 devices in a mesh: fsdp: 8 (over y, x, core), dp: 4 (over z).
Axes of the slice: x: 2, y: 2, z: 4, core: 2. Of those that a mesh axis runs over, the one named last changes fastest.
Arguments:
- hidden: bfloat16 [6144, 8192], P('fsdp', 'dp'), may hold values from -6 to 6
- combine_weight: float32 [6144], P('fsdp'), may hold values from 0.2 to 1
- down_weight: bfloat16 [4096, 2, 8192], P('fsdp', None, 'dp'), may hold values from -0.0625 to 0.0625
- cotangent: bfloat16 [6144, 4096], P('fsdp', 'dp'), may hold values from -6 to 6
- expert_rows: int32 [8, 2], P('fsdp'), may hold values from 1 to 640, as said below
- block_expert: int32 [48], P('fsdp'), may hold values from 0 to 1, as said below
- slot_token: int32 [6144], P('fsdp'), may hold values from 0 to 767, as said below
Outputs:
- expert_out: bfloat16 [6144, 4096], P('fsdp', 'dp')
- grad_hidden: bfloat16 [6144, 8192], P('fsdp', 'dp')
- grad_down: bfloat16 [4096, 2, 8192], P('fsdp', None, 'dp')
The draws below stay inside these ranges and needn't reach their ends.
Inputs may be any that keep to these rules, and one draw needn't show every extreme that they name: `expert_rows`: row i gives the live rows of the first and the second expert in group i; the first expert's rows fill blocks from block 0 on, the second's start at the next free block, each takes ceil(rows / 128) blocks and both together at most 6; in every draw some group uses all 6 blocks. `block_expert`: within each group: 0 for the first expert's blocks, 1 for every later block; blocks past both experts' have no live rows. `slot_token`: tokens counted within the slot's group; the live slots of one expert in a group name different tokens of that group; slots that are not live hold arbitrary tokens.
All inputs are finite; a program needn't handle non-finite values.
Results may differ from the reference program's by a relative error of at most 0.014.
Values may be sent and summed in bfloat16 or wider, within the bound.
A program may use at most 192 MiB of HBM per device.

```python
import math
import jax
import jax.numpy as jnp
from jax import lax

D = 4096
FF = 8192
EXPERTS = 2
BLK = 128
NB_DEV = 6
SLOTS = 6144
TOKENS = 6144
BLOCKS = 48
N_FSDP = 8
N_DP = 4


def layout(key):
    group_total = BLOCKS // NB_DEV
    slot_total = NB_DEV * BLK
    fuller = jax.random.randint(jax.random.fold_in(key, 11), (), 0, group_total)

    def single(group_index):
        subkey = jax.random.fold_in(jax.random.fold_in(key, 17), group_index)
        keys = jax.random.split(subkey, 6)
        is_full = group_index == fuller
        first_blocks = jax.random.randint(keys[0], (), 1, NB_DEV)
        second_blocks = jax.random.randint(keys[1], (), 1, NB_DEV - first_blocks + 1)
        first_blocks = jnp.where(is_full, NB_DEV - 1, first_blocks)
        second_blocks = jnp.where(is_full, 1, second_blocks)
        first_rows = (first_blocks - 1) * BLK + jax.random.randint(keys[2], (), 1, BLK + 1)
        first_rows = jnp.where(is_full, first_blocks * BLK, first_rows)
        second_rows = (second_blocks - 1) * BLK + jax.random.randint(keys[3], (), 1, BLK + 1)
        order_first = jax.random.permutation(keys[4], slot_total)
        order_second = jax.random.permutation(keys[5], slot_total)
        positions = jnp.arange(slot_total, dtype=jnp.int32)
        later = jnp.clip(positions - first_blocks * BLK, 0, slot_total - 1)
        tokens = jnp.where(positions < first_blocks * BLK, order_first[positions], order_second[later])
        tokens = jnp.where(is_full, order_first[positions], tokens)
        experts = jnp.where(jnp.arange(NB_DEV, dtype=jnp.int32) < first_blocks, 0, 1)
        rows_pair = jnp.stack([first_rows, second_rows])
        return (rows_pair.astype(jnp.int32), experts.astype(jnp.int32), tokens.astype(jnp.int32))
    return jax.vmap(single)(jnp.arange(group_total, dtype=jnp.int32))


def draw_expert_rows(key, part):
    return layout(key)[0]


def draw_block_expert(key, part):
    return layout(key)[1].reshape(-1)


def draw_slot_token(key, part):
    return layout(key)[2].reshape(-1)


def steps_of(own_key, shape, cuts, low, high):
    loudness, own = 1.0, jax.random.fold_in(own_key, 6)
    for dim, blocks in cuts:
        draws = jnp.exp(jax.random.uniform(jax.random.fold_in(own, dim), (blocks,), jnp.float32, low / len(cuts), high / len(cuts)))
        loudness = loudness * jnp.repeat(draws, shape[dim] // blocks).reshape([-1 if axis == dim else 1 for axis in range(len(shape))])
    return loudness


def noise(rng, dims, spread, most, pieces=(), kind=jnp.bfloat16):
    factor_of = steps_of(rng, dims, pieces, -0.22, 0.18) if pieces else 1.0
    result = jax.random.normal(rng, dims, jnp.float32) * spread * factor_of
    return jnp.minimum(jnp.maximum(result, -most), most).astype(kind)


def setup_inputs(seed: int = 0) -> dict:
    arg_keys = jax.random.split(jax.random.key(seed), 8)
    return {
        "hidden": noise(arg_keys[0], (SLOTS, FF), 1.0, 6.0, ((0, 8), (1, 4))),
        "combine_weight": jnp.clip(0.2 + 0.8 * jax.random.uniform(arg_keys[1], (SLOTS,), jnp.float32) ** steps_of(arg_keys[1], (SLOTS,), ((0, 8),), -0.2, 0.2), 0.2, 1.0),
        "down_weight": noise(arg_keys[2], (D, EXPERTS, FF), FF ** -0.5, 0.0625, ((0, 8), (2, 4))),
        "cotangent": noise(arg_keys[3], (TOKENS, D), 1.0, 6.0, ((0, 8), (1, 4))),
        "expert_rows": draw_expert_rows(jax.random.fold_in(arg_keys[7], 71), 0),
        "block_expert": draw_block_expert(jax.random.fold_in(arg_keys[7], 71), 0),
        "slot_token": draw_slot_token(jax.random.fold_in(arg_keys[7], 71), 0),
    }


def reference(hidden, combine_weight, down_weight, cotangent, expert_rows, block_expert, slot_token):
    group_count = N_FSDP
    hidden_groups = N_DP
    slot_count = NB_DEV * BLK
    group_width = FF // hidden_groups
    positions = jnp.arange(slot_count, dtype=jnp.int32)
    blocks = positions // BLK
    expert_ids = jnp.arange(EXPERTS, dtype=jnp.int32)

    def per_group(running, group_index):
        live_rows = lax.dynamic_index_in_dim(expert_rows, group_index, 0, keepdims=False)
        first_blocks = (live_rows[0] + BLK - 1) // BLK
        second_blocks = (live_rows[1] + BLK - 1) // BLK
        live = jnp.where(blocks < first_blocks, positions < live_rows[0], (blocks < first_blocks + second_blocks) & (positions - first_blocks * BLK < live_rows[1]))
        offset = (group_index * slot_count).astype(jnp.int32)
        hid_rows = lax.dynamic_slice_in_dim(hidden, offset, slot_count, 0)
        slot_scale = lax.dynamic_slice_in_dim(combine_weight, offset, slot_count, 0) * live.astype(jnp.float32)
        tokens = lax.dynamic_slice_in_dim(slot_token, offset, slot_count, 0)
        experts = lax.dynamic_slice_in_dim(block_expert, (group_index * NB_DEV).astype(jnp.int32), NB_DEV, 0)
        cot_rows = lax.dynamic_slice_in_dim(cotangent, offset, slot_count, 0)
        slot_cot = (slot_scale[:, None] * cot_rows[tokens].astype(jnp.float32)).astype(jnp.bfloat16)
        panels = jnp.take(down_weight, experts, axis=1)
        hid_split = hid_rows.reshape(NB_DEV, BLK, hidden_groups, group_width).astype(jnp.float32)
        panel_split = panels.reshape(D, NB_DEV, hidden_groups, group_width).astype(jnp.float32)
        slot_out = jnp.einsum('btjh,dbjh->jbtd', hid_split, panel_split).reshape(hidden_groups, slot_count, D)

        def combine(part_out):
            return jnp.zeros((slot_count, D), jnp.float32).at[tokens].add(slot_scale[:, None] * part_out)
        token_part = jax.vmap(combine)(slot_out).astype(jnp.bfloat16)
        token_part = lax.optimization_barrier(token_part)
        expert_out = lax.optimization_barrier(jnp.sum(token_part.astype(jnp.float32), axis=0)).astype(jnp.bfloat16)
        cot_blocks = slot_cot.reshape(NB_DEV, BLK, D).astype(jnp.float32)
        grad_hidden = jnp.einsum('btd,dbf->btf', cot_blocks, panels.astype(jnp.float32)).reshape(slot_count, FF)
        products = jnp.einsum('btd,btf->bdf', cot_blocks, hid_rows.reshape(NB_DEV, BLK, FF).astype(jnp.float32))
        onehot = (experts[:, None] == expert_ids[None, :]).astype(jnp.float32)
        device_grad = jnp.einsum('be,bdf->def', onehot, products, precision=lax.Precision.HIGHEST)
        device_grad = lax.optimization_barrier(device_grad.astype(jnp.bfloat16))
        running = running + device_grad.astype(jnp.float32)
        return (running, (expert_out, grad_hidden.astype(jnp.bfloat16)))
    start_grad = jnp.zeros((D, EXPERTS, FF), jnp.float32)
    summed, (outputs, hidden_grads) = lax.scan(per_group, start_grad, jnp.arange(group_count, dtype=jnp.int32))
    grad_down = (summed * (1.0 / math.sqrt(SLOTS))).astype(jnp.bfloat16)
    return (outputs.reshape(TOKENS, D), hidden_grads.reshape(SLOTS, FF), grad_down)
```

```python
import functools
import math

import jax
import jax.numpy as jnp
from jax import lax
from jax.experimental import pallas as pl
from jax.experimental.pallas import tpu as pltpu
from jax.sharding import PartitionSpec as P

EXPERTS = 2
BLK = 128
VMEM_LIMIT = 48 * 1024 * 1024


def line_gather(x, axis):
    n = lax.axis_size(axis)
    me = lax.axis_index(axis)
    right, left = [x], [x]
    for s in range(1, n):
        right.append(lax.ppermute(right[-1], axis, [(i, i + 1) for i in range(s - 1, n - 1)]))
        left.append(lax.ppermute(left[-1], axis, [(i, i - 1) for i in range(1, n - s + 1)]))
    buf = jnp.zeros((n,) + x.shape, x.dtype)
    for s in range(n):
        piece = x if s == 0 else jnp.where(me >= s, right[s], left[n - s])
        buf = lax.dynamic_update_index_in_dim(buf, piece, lax.rem(me - s + n, n), 0)
    return buf


def line_scatter(parts, axis):
    n = lax.axis_size(axis)
    me = lax.axis_index(axis)

    def term(j):
        return lax.dynamic_index_in_dim(parts, lax.rem(j + n, n), 0, keepdims=False).astype(jnp.float32)

    total = term(me)
    from_left = from_right = None
    for s in range(1, n):
        up, down = term(me + n - s), term(me - n + s)
        if from_left is not None:
            up, down = up + from_left.astype(jnp.float32), down + from_right.astype(jnp.float32)
        from_left = lax.ppermute(up.astype(parts.dtype), axis, [(i, i + 1) for i in range(s)])
        from_right = lax.ppermute(
            down.astype(parts.dtype), axis, [(i, i - 1) for i in range(n - s, n)]
        )
    if from_left is not None:
        total = total + from_left.astype(jnp.float32) + from_right.astype(jnp.float32)
    return total.astype(parts.dtype)


def slot_cot_kernel(tok_ref, scale_ref, cot_ref, out_ref):
    slots, tokens = tok_ref.shape[0], cot_ref.shape[1]
    pick = tok_ref[...] == lax.broadcasted_iota(jnp.int32, (slots, tokens), 1)
    pick = pick.astype(jnp.float32).astype(jnp.bfloat16)
    rows = jnp.dot(pick, cot_ref[0], preferred_element_type=jnp.float32)
    out_ref[...] = (scale_ref[...] * rows).astype(jnp.bfloat16)


def make_slot_cot(slot_token, slot_scale, cot_slabs):
    n, tokens, width = cot_slabs.shape
    slots = slot_token.shape[0]
    return pl.pallas_call(
        slot_cot_kernel,
        grid=(n,),
        in_specs=[
            pl.BlockSpec((slots, 1), lambda j: (0, 0)),
            pl.BlockSpec((slots, 1), lambda j: (0, 0)),
            pl.BlockSpec((1, tokens, width), lambda j: (j, 0, 0)),
        ],
        out_specs=pl.BlockSpec((slots, width), lambda j: (0, j)),
        out_shape=jax.ShapeDtypeStruct((slots, n * width), jnp.bfloat16),
        compiler_params=pltpu.CompilerParams(vmem_limit_bytes=VMEM_LIMIT),
        cost_estimate=pl.CostEstimate(
            flops=2 * slots * tokens * n * width, bytes_accessed=4 * slots * n * width, transcendentals=0
        ),
        name="slot_cot",
    )(slot_token[:, None], slot_scale[:, None], cot_slabs)


def grouped(expert_ref, w_ref, blocks, one):
    start = 0
    while start < blocks:
        first = expert_ref[start]
        if start + 1 < blocks:
            second = expert_ref[start + 1]
            both = first == second

            @pl.when(both)
            def _():
                one(start * BLK, 2 * BLK, w_ref[first])

            @pl.when(jnp.logical_not(both))
            def _():
                one(start * BLK, BLK, w_ref[first])
                one((start + 1) * BLK, BLK, w_ref[second])

            start += 2
        else:
            one(start * BLK, BLK, w_ref[first])
            start += 1


def forward_kernel(blocks, expert_ref, tok_ref, scale_ref, hid_ref, w_ref, out_ref, scaled):
    def one(row, count, w):
        rows = pl.ds(row, count)
        out = lax.dot_general(
            hid_ref[rows, :], w, (((1,), (1,)), ((), ())), preferred_element_type=jnp.float32
        )
        scaled[rows, :] = (scale_ref[rows, :] * out).astype(jnp.bfloat16)

    grouped(expert_ref, w_ref, blocks, one)
    tokens, slots = out_ref.shape[1], tok_ref.shape[1]
    put = tok_ref[...] == lax.broadcasted_iota(jnp.int32, (tokens, slots), 0)
    put = put.astype(jnp.float32).astype(jnp.bfloat16)
    out_ref[0] = jnp.dot(put, scaled[...], preferred_element_type=jnp.float32).astype(jnp.bfloat16)


def forward(block_expert, slot_token, slot_scale, hidden, panel, tokens, n):
    slots, width = hidden.shape
    model = panel.shape[1]
    part = model // n
    tile = min(512, part)
    per = part // tile
    return pl.pallas_call(
        functools.partial(forward_kernel, slots // BLK),
        grid_spec=pltpu.PrefetchScalarGridSpec(
            num_scalar_prefetch=1,
            grid=(model // tile,),
            in_specs=[
                pl.BlockSpec((1, slots), lambda d, e: (0, 0)),
                pl.BlockSpec((slots, 1), lambda d, e: (0, 0)),
                pl.BlockSpec((slots, width), lambda d, e: (0, 0)),
                pl.BlockSpec((EXPERTS, tile, width), lambda d, e: (0, d, 0)),
            ],
            out_specs=pl.BlockSpec((1, tokens, tile), lambda d, e: (d // per, 0, d % per)),
            scratch_shapes=[pltpu.VMEM((slots, tile), jnp.bfloat16)],
        ),
        out_shape=jax.ShapeDtypeStruct((n, tokens, part), jnp.bfloat16),
        compiler_params=pltpu.CompilerParams(vmem_limit_bytes=VMEM_LIMIT),
        cost_estimate=pl.CostEstimate(
            flops=2 * slots * model * (width + tokens),
            bytes_accessed=2 * EXPERTS * model * width,
            transcendentals=0,
        ),
        name="expert_forward",
    )(block_expert, slot_token[None, :], slot_scale[:, None], hidden, panel)


def hidden_grad_kernel(blocks, expert_ref, cot_ref, w_ref, out_ref):
    def one(row, count, w):
        rows = pl.ds(row, count)
        out_ref[rows, :] = jnp.dot(
            cot_ref[rows, :], w, preferred_element_type=jnp.float32
        ).astype(jnp.bfloat16)

    grouped(expert_ref, w_ref, blocks, one)


def hidden_grad(block_expert, slot_cot, panel):
    slots, model = slot_cot.shape
    width = panel.shape[2]
    tile = min(256, width)
    return pl.pallas_call(
        functools.partial(hidden_grad_kernel, slots // BLK),
        grid_spec=pltpu.PrefetchScalarGridSpec(
            num_scalar_prefetch=1,
            grid=(width // tile,),
            in_specs=[
                pl.BlockSpec((slots, model), lambda h, e: (0, 0)),
                pl.BlockSpec((EXPERTS, model, tile), lambda h, e: (0, 0, h)),
            ],
            out_specs=pl.BlockSpec((slots, tile), lambda h, e: (0, h)),
        ),
        out_shape=jax.ShapeDtypeStruct((slots, width), jnp.bfloat16),
        compiler_params=pltpu.CompilerParams(vmem_limit_bytes=VMEM_LIMIT),
        cost_estimate=pl.CostEstimate(
            flops=2 * slots * model * width,
            bytes_accessed=2 * EXPERTS * model * width,
            transcendentals=0,
        ),
        name="hidden_grad",
    )(block_expert, slot_cot, panel)


def weight_grad_kernel(blocks, first_ref, cot_ref, hid_ref, out_ref):
    width = hid_ref.shape[1]
    step = min(512, width)

    def one(expert, lo, hi, col):
        out_ref[expert, :, col : col + step] = lax.dot_general(
            cot_ref[lo:hi, :],
            hid_ref[lo:hi, col : col + step],
            (((0,), (0,)), ((), ())),
            preferred_element_type=jnp.float32,
        ).astype(jnp.bfloat16)

    for count in range(1, blocks):

        @pl.when(first_ref[0] == count)
        def _():
            for col in range(0, width, step):
                one(0, 0, count * BLK, col)
                one(1, count * BLK, blocks * BLK, col)


def weight_grad(block_expert, slot_cot, hidden):
    slots, model = slot_cot.shape
    width = hidden.shape[1]
    tile = min(512, model)
    first_blocks = jnp.sum((block_expert == 0).astype(jnp.int32)).reshape(1)
    return pl.pallas_call(
        functools.partial(weight_grad_kernel, slots // BLK),
        grid_spec=pltpu.PrefetchScalarGridSpec(
            num_scalar_prefetch=1,
            grid=(model // tile,),
            in_specs=[
                pl.BlockSpec((slots, tile), lambda d, e: (0, d)),
                pl.BlockSpec((slots, width), lambda d, e: (0, 0)),
            ],
            out_specs=pl.BlockSpec((EXPERTS, tile, width), lambda d, e: (0, d, 0)),
        ),
        out_shape=jax.ShapeDtypeStruct((EXPERTS, model, width), jnp.bfloat16),
        compiler_params=pltpu.CompilerParams(vmem_limit_bytes=VMEM_LIMIT),
        cost_estimate=pl.CostEstimate(
            flops=2 * slots * model * width,
            bytes_accessed=2 * EXPERTS * model * width,
            transcendentals=0,
        ),
        name="weight_grad",
    )(first_blocks, slot_cot, hidden)


def local(hidden, combine_weight, down_weight, cotangent, expert_rows, block_expert, slot_token):
    slot_count = hidden.shape[0]
    token_count = cotangent.shape[0]
    n = lax.axis_size("dp")
    positions = jnp.arange(slot_count, dtype=jnp.int32)
    blocks = positions // BLK
    live_rows = expert_rows[0]
    first_blocks = (live_rows[0] + BLK - 1) // BLK
    second_blocks = (live_rows[1] + BLK - 1) // BLK
    live = jnp.where(
        blocks < first_blocks,
        positions < live_rows[0],
        (blocks < first_blocks + second_blocks) & (positions - first_blocks * BLK < live_rows[1]),
    )
    slot_scale = combine_weight * live.astype(jnp.float32)
    panel = lax.all_gather(jnp.swapaxes(down_weight, 0, 1), "fsdp", axis=1, tiled=True)
    cot_slabs = line_gather(cotangent, "dp")
    slot_cot = make_slot_cot(slot_token, slot_scale, cot_slabs)
    parts = weight_grad(block_expert, slot_cot, hidden)
    sums = lax.psum_scatter(parts, "fsdp", scatter_dimension=1, tiled=True)
    token_parts = forward(block_expert, slot_token, slot_scale, hidden, panel, token_count, n)
    expert_out = line_scatter(token_parts, "dp")
    grad_hidden = hidden_grad(block_expert, slot_cot, panel)
    expert_out, grad_hidden, sums = lax.optimization_barrier((expert_out, grad_hidden, sums))
    grad_scale = 1.0 / math.sqrt(lax.axis_size("fsdp") * slot_count)
    grad_down = (jnp.swapaxes(sums, 0, 1).astype(jnp.float32) * grad_scale).astype(jnp.bfloat16)
    return (expert_out, grad_hidden, grad_down)


def solution(mesh):
    in_specs = (
        P("fsdp", "dp"),
        P("fsdp"),
        P("fsdp", None, "dp"),
        P("fsdp", "dp"),
        P("fsdp", None),
        P("fsdp"),
        P("fsdp"),
    )
    out_specs = (P("fsdp", "dp"), P("fsdp", "dp"), P("fsdp", None, "dp"))
    return jax.shard_map(local, mesh=mesh, in_specs=in_specs, out_specs=out_specs, check_vma=False)
```
